32 devices in a mesh: groups: 2 (over y), seq: 4 (over z), tensor: 4 (over x, core).
Axes of the slice: x: 2, y: 2, z: 4, core: 2. Of those that a mesh axis runs over, the one named last changes fastest.
Arguments:
- queries: bfloat16 [2048, 3072], P(('groups', 'seq'), 'tensor'), parts along dimension 0, may hold values from -8 to 8
- keys: bfloat16 [2048, 3072], P(('groups', 'seq'), 'tensor'), parts along dimension 0, may hold values from -6 to 6
- values: bfloat16 [2048, 3072], P(('groups', 'seq'), 'tensor'), parts along dimension 0, may hold values from -110 to 110
- text_keys: bfloat16 [128, 3072], P(('groups', 'seq'), 'tensor'), parts along dimension 0, may hold values from -9 to 9
- text_values: bfloat16 [128, 3072], P(('groups', 'seq'), 'tensor'), parts along dimension 0, may hold values from -24 to 24
- text_len: int32 [2], P('groups'), parts along dimension 0, may hold values from 1 to 64
- uncond: bfloat16 [2048, 3072], P(('groups', 'seq'), 'tensor'), parts along dimension 0, may hold values from -10 to 10
- flags: int32 [2048], P(('groups', 'seq')), parts along dimension 0, may hold values 0 or 1
- guide_num: int32 [2], P('groups'), parts along dimension 0, may hold values from 768 to 2559
- guide_den: int32 [2], P('groups'), parts along dimension 0, may hold values from 512 to 1087
Outputs:
- guided: bfloat16 [2048, 3072], P(('groups', 'seq'), 'tensor'), parts along dimension 0
The draws below stay inside these ranges and needn't reach their ends.
There are 2 independent parts, one for each index of `groups`. The reference program is written for one: setup_inputs(seed, part) draws one part's arguments, and reference() takes and returns one part's arrays. A program takes and returns all parts, laid end to end along the dimension named above; each array names one. Nothing has to cross between parts.
All inputs are finite; a program needn't handle non-finite values. No bound on the sum of `flags` on one device may be relied on, other than what follows from the above.
Results may differ from the reference program's by a relative error of at most 0.0045.
Values may be sent and summed in bfloat16 or wider, within the bound.
A program may use at most 64 MiB of HBM per device.

```python
import math
import jax
import jax.numpy as jnp
from jax import lax

HEADS = 24
HEAD_DIM = 128
TOKENS = 1024
TXT = 64
HW = 3072


def head_ramp(top):
    column = jnp.arange(HEADS * HEAD_DIM) // HEAD_DIM
    frac = column.astype(jnp.float32) / max(HEADS - 1, 1)
    return top ** frac


def head_frac():
    column = jnp.arange(HEADS * HEAD_DIM) // HEAD_DIM
    return column.astype(jnp.float32) / max(HEADS - 1, 1)


def column_mean(key):
    first, second = jax.random.split(jax.random.fold_in(key, 202))
    signs = jnp.where(jax.random.normal(first, (HEADS * HEAD_DIM,)) > 0, 1.0, -1.0)
    sizes = jax.random.uniform(second, (HEADS * HEAD_DIM,), minval=0.75, maxval=1.25)
    return signs * sizes


def draw_queries(key, part):
    key = jax.random.fold_in(key, 1)
    drawn = jnp.clip(2.0 * jax.random.normal(key, (TOKENS, HEADS * HEAD_DIM)), -8.0, 8.0)
    return drawn.astype(jnp.bfloat16)


def draw_keys(key, part):
    key = jax.random.fold_in(key, 2)
    drawn = jnp.clip(jax.random.normal(key, (TOKENS, HEADS * HEAD_DIM)), -6.0, 6.0)
    return drawn.astype(jnp.bfloat16)


def draw_values(key, part):
    mean = column_mean(key)
    key = jax.random.fold_in(key, 3)
    drawn = jnp.clip(jax.random.normal(key, (TOKENS, HEADS * HEAD_DIM)), -3.0, 3.0) * 4.0
    drawn = drawn * head_ramp(3.0)[None, :]
    return (drawn + mean[None, :]).astype(jnp.bfloat16)


def draw_uncond(key, part):
    mean = column_mean(key)
    key = jax.random.fold_in(key, 4)
    drawn = jnp.clip(jax.random.normal(key, (TOKENS, HEADS * HEAD_DIM)), -3.0, 3.0) * 0.25
    drawn = drawn * head_ramp(3.0)[None, :]
    gain = 2.0 * head_frac()
    return (drawn + (gain * mean)[None, :]).astype(jnp.bfloat16)


def place_ends(values, rng, smallest, high):
    index_at = [jax.random.randint(jax.random.fold_in(rng, axis), (), 0, length) for axis, length in enumerate(values.shape)]
    longest = values.shape.index(max(values.shape))
    beside = index_at[:longest] + [(index_at[longest] + 1) % values.shape[longest]] + index_at[longest + 1:]
    return values.at[tuple(index_at)].set(smallest).at[tuple(beside)].set(high)


def steps_of(key, extent, shards, least, top_value):
    def one(axis_at, blocks):
        draws = jax.random.uniform(jax.random.fold_in(jax.random.fold_in(key, 6), axis_at), (blocks,), jnp.float32, least / len(shards), top_value / len(shards))
        return jnp.repeat(jnp.exp(draws), extent[axis_at] // blocks).reshape((-1,) + (1,) * (len(extent) - axis_at - 1))

    level = one(*shards[0])
    for cut in shards[1:]:
        level = level * one(*cut)
    return level


def centred(rng, extent, deviation, limit, cuts=(), held_as=jnp.bfloat16):
    factor_of = steps_of(rng, extent, cuts, -0.22, 0.18) if cuts else 1.0
    result = jax.random.normal(rng, extent, jnp.float32) * deviation * factor_of
    return jnp.minimum(jnp.maximum(result, -limit), limit).astype(held_as)


def setup_inputs(seed: int = 0, part: int = 0) -> dict:
    arg_keys = jax.random.split(jax.random.key(seed), 11)
    part_keys = jax.random.split(jax.random.fold_in(arg_keys[10], part), 11)
    return {
        "queries": draw_queries(jax.random.fold_in(jax.random.fold_in(arg_keys[10], part), 71), part),
        "keys": draw_keys(jax.random.fold_in(jax.random.fold_in(arg_keys[10], part), 71), part),
        "values": draw_values(jax.random.fold_in(jax.random.fold_in(arg_keys[10], part), 71), part),
        "text_keys": centred(part_keys[3], (TXT, HW), 1.5, 9.0, ((0, 4), (1, 4))),
        "text_values": centred(part_keys[4], (TXT, HW), 4.0, 24.0, ((0, 4), (1, 4))),
        "text_len": jax.random.randint(part_keys[5], (1,), 1, TXT + 1).astype(jnp.int32),
        "uncond": draw_uncond(jax.random.fold_in(jax.random.fold_in(arg_keys[10], part), 71), part),
        "flags": place_ends((jax.random.randint(part_keys[7], (TOKENS,), 0, 4) < 3).astype(jnp.int32), jax.random.fold_in(part_keys[7], 1), 0, 1),
        "guide_num": jax.random.randint(part_keys[8], (1,), 768, 2560).astype(jnp.int32),
        "guide_den": jax.random.randint(part_keys[9], (1,), 512, 1088).astype(jnp.int32),
    }


def reference(queries, keys, values, text_keys, text_values, text_len, uncond, flags, guide_num, guide_den):
    image_rows = keys.shape[0]
    joint_keys = jnp.concatenate([keys, text_keys], axis=0)
    joint_values = jnp.concatenate([values, text_values], axis=0)
    count = joint_keys.shape[0]
    position = jnp.arange(count).astype(jnp.int32)
    live = (position < image_rows) | (position - image_rows < text_len[0])
    factor = 1.0 / math.sqrt(HEAD_DIM)
    query_heads = queries.reshape(image_rows, HEADS, HEAD_DIM).transpose(1, 0, 2)
    key_heads = joint_keys.reshape(count, HEADS, HEAD_DIM).transpose(1, 0, 2)
    value_heads = joint_values.reshape(count, HEADS, HEAD_DIM).transpose(1, 0, 2)

    def one_head(operands):
        query_block, key_block, value_block = operands
        scores = jnp.dot(query_block, key_block.T, preferred_element_type=jnp.float32) * factor
        scores = jnp.where(live[None, :], scores, -1e+30)
        top = lax.optimization_barrier(jnp.max(scores, axis=1, keepdims=True))
        weights = jnp.exp(scores - top)
        total = lax.optimization_barrier(jnp.sum(weights, axis=1, keepdims=True))
        mixed = jnp.dot(weights.astype(jnp.bfloat16), value_block, preferred_element_type=jnp.float32)
        return mixed / total
    per_head = lax.map(one_head, (query_heads, key_heads, value_heads))
    cond = per_head.transpose(1, 0, 2).reshape(image_rows, HEADS * HEAD_DIM)
    diff = cond - uncond.astype(jnp.float32)
    inner = lax.optimization_barrier(jnp.sum(diff * cond, axis=1))
    square = lax.optimization_barrier(jnp.sum(cond * cond, axis=1))
    width = HEADS * HEAD_DIM
    coef = inner / width / (square / width + 1e-06)
    scale = guide_num[0].astype(jnp.float32) / guide_den[0].astype(jnp.float32)
    steered = cond + (scale - 1.0) * (diff - coef[:, None] * cond)
    return jnp.where(flags[:, None] > 0, steered, cond).astype(jnp.bfloat16)
```

```python
import functools
import math

import jax
import jax.numpy as jnp
from jax import lax
from jax.experimental import pallas as pl
from jax.experimental.pallas import tpu as pltpu
from jax.sharding import PartitionSpec as P

HEAD_DIM = 128
SEQ = 4
OWN_HEADS = 6
MESH = pl.DeviceIdType.MESH
K, V, TK, TV, Q = range(5)


def kernel(
    tensor_size,
    q_hbm, k_hbm, v_hbm, tk_hbm, tv_hbm, len_ref, uncond_ref, flags_ref, num_ref, den_ref,
    out_ref,
    qs, ks, vs, cond, sums, stats,
    own_sem, send_sem, recv_sem, back_send, back_recv, stat_send, stat_recv,
):
    rows = q_hbm.shape[0]
    text_rows = tk_hbm.shape[0]
    tokens = SEQ * rows
    group = lax.axis_index("groups")
    z = lax.axis_index("seq")
    t = lax.axis_index("tensor")
    core = lax.rem(t, 2)
    half = z // 2
    peers = (lax.rem(z + 2, SEQ), SEQ - 1 - z, z + 1 - 2 * lax.rem(z, 2))
    has_extra = lax.rem(z, 2) == core

    def at(seq, tensor):
        return (group, seq, tensor)

    sources = {K: k_hbm, V: v_hbm, TK: tk_hbm, TV: tv_hbm, Q: q_hbm}

    def place(kind, slot, source):
        if kind == Q:
            return qs.at[slot, pl.ds(source * rows, rows), :]
        big = ks if kind in (K, TK) else vs
        if kind in (K, V):
            return big.at[slot, pl.ds(source * rows, rows), :]
        return big.at[slot, pl.ds(tokens + source * text_rows, text_rows), :]

    def column(head):
        return pl.ds(pl.multiple_of(head * HEAD_DIM, HEAD_DIM), HEAD_DIM)

    def push(kind, slot, head, target):
        return pltpu.make_async_remote_copy(
            src_ref=sources[kind].at[:, column(head)],
            dst_ref=place(kind, slot, z),
            send_sem=send_sem.at[slot, kind, target],
            recv_sem=recv_sem.at[slot, kind, z],
            device_id=at(target, t),
            device_id_type=MESH,
        )

    def arrival(kind, slot, source):
        return pltpu.make_async_remote_copy(
            src_ref=place(kind, slot, source),
            dst_ref=place(kind, slot, source),
            send_sem=send_sem.at[slot, kind, source],
            recv_sem=recv_sem.at[slot, kind, source],
            device_id=at(source, t),
            device_id_type=MESH,
        )

    def keep(kind, slot, head):
        return pltpu.make_async_copy(
            sources[kind].at[:, column(head)], place(kind, slot, z), own_sem.at[slot, kind]
        )

    def give_back(slot, head, target):
        return pltpu.make_async_remote_copy(
            src_ref=qs.at[slot, pl.ds(target * rows, rows), :],
            dst_ref=cond.at[head],
            send_sem=back_send.at[slot, target],
            recv_sem=back_recv.at[head],
            device_id=at(target, t),
            device_id_type=MESH,
        )

    kinds = (K, TK, V, TV, Q)
    for kind in kinds:
        keep(kind, 0, z).start()

    @pl.when(has_extra)
    def _():
        for kind in kinds:
            keep(kind, 1, SEQ + half).start()

    barrier = pltpu.get_barrier_semaphore()
    for peer in peers:
        pl.semaphore_signal(barrier, inc=1, device_id=at(peer, t), device_id_type=MESH)
    others = [lax.rem(t + step, tensor_size) for step in range(1, tensor_size)]
    for other in others:
        pl.semaphore_signal(barrier, inc=1, device_id=at(z, other), device_id_type=MESH)
    pl.semaphore_wait(barrier, len(peers) + len(others))

    far = 2 * (1 - half) + core
    near = 2 * half + core
    for kind in kinds:
        push(kind, 1, SEQ + 1 - half, far).start()

        @pl.when(jnp.logical_not(has_extra))
        def _():
            push(kind, 1, SEQ + half, near).start()

    for kind in kinds:
        for peer in peers:
            push(kind, 0, peer, peer).start()

    scale_log2 = math.log2(math.e) / math.sqrt(HEAD_DIM)
    live = lax.broadcasted_iota(jnp.int32, (rows, SEQ * text_rows), 1) < len_ref[0]
    contract = (((1,), (1,)), ((), ()))

    def attend(slot, source, head):
        query = qs[slot, pl.ds(source * rows, rows), :]
        image = lax.dot_general(
            query, ks[slot, pl.ds(0, tokens), :], contract, preferred_element_type=jnp.float32
        )
        text = lax.dot_general(
            query,
            ks[slot, pl.ds(tokens, SEQ * text_rows), :],
            contract,
            preferred_element_type=jnp.float32,
        )
        text = jnp.where(live, text * scale_log2, -1e30)
        image = image * scale_log2
        top = jnp.maximum(
            jnp.max(image, axis=1, keepdims=True), jnp.max(text, axis=1, keepdims=True)
        )
        image = jnp.exp2(image - top)
        text = jnp.exp2(text - top)
        total = jnp.sum(image, axis=1, keepdims=True) + jnp.sum(text, axis=1, keepdims=True)
        mixed = jnp.dot(
            image.astype(jnp.bfloat16),
            vs[slot, pl.ds(0, tokens), :],
            preferred_element_type=jnp.float32,
        ) + jnp.dot(
            text.astype(jnp.bfloat16),
            vs[slot, pl.ds(tokens, SEQ * text_rows), :],
            preferred_element_type=jnp.float32,
        )
        return (mixed / total).astype(jnp.bfloat16)

    def work(slot, head):
        for kind in (K, TK, V, TV):
            keep(kind, slot, head).wait()
            for peer in peers:
                arrival(kind, slot, peer).wait_recv()
        keep(Q, slot, head).wait()
        cond[head] = attend(slot, z, head)
        for peer in peers:
            arrival(Q, slot, peer).wait_recv()
            result = attend(slot, peer, head)
            qs[slot, pl.ds(peer * rows, rows), :] = result
            give_back(slot, head, peer).start()

    @pl.when(has_extra)
    def _():
        work(1, SEQ + half)

    work(0, z)

    def landed(head, source):
        return pltpu.make_async_remote_copy(
            src_ref=cond.at[head],
            dst_ref=cond.at[head],
            send_sem=back_send.at[0, source],
            recv_sem=back_recv.at[head],
            device_id=at(source, t),
            device_id_type=MESH,
        )

    landed(SEQ + 1 - half, far).wait_recv()

    @pl.when(jnp.logical_not(has_extra))
    def _():
        landed(SEQ + half, near).wait_recv()

    for peer in peers:
        landed(peer, peer).wait_recv()

    inner = jnp.zeros((rows, HEAD_DIM), jnp.float32)
    square = jnp.zeros((rows, HEAD_DIM), jnp.float32)
    for head in range(OWN_HEADS):
        mine = cond[head].astype(jnp.float32)
        diff = mine - uncond_ref[:, head * HEAD_DIM : (head + 1) * HEAD_DIM].astype(jnp.float32)
        inner += diff * mine
        square += mine * mine
    lane = lax.broadcasted_iota(jnp.int32, (rows, HEAD_DIM), 1)
    pair = jnp.where(
        lane == 0,
        jnp.sum(inner, axis=1, keepdims=True),
        jnp.sum(square, axis=1, keepdims=True),
    )
    sums[...] = pair.T[0:8, :]

    def tell(step):
        return pltpu.make_async_remote_copy(
            src_ref=sums,
            dst_ref=stats.at[step - 1],
            send_sem=stat_send.at[step - 1],
            recv_sem=stat_recv.at[step - 1],
            device_id=at(z, lax.rem(t + step, tensor_size)),
            device_id_type=MESH,
        )

    for step in range(1, tensor_size):
        tell(step).start()
    both = sums[...]
    for step in range(1, tensor_size):
        tell(step).wait_recv()
        both = both + stats[step - 1]
    width = tensor_size * OWN_HEADS * HEAD_DIM
    coef = both[0:1, :] / width / (both[1:2, :] / width + 1e-6)
    scale = num_ref[0].astype(jnp.float32) / den_ref[0].astype(jnp.float32)
    alpha = jnp.where(flags_ref[...] > 0, scale - 1.0, 0.0)
    line = lax.broadcasted_iota(jnp.int32, (HEAD_DIM, rows), 0)
    columns = jnp.where(line == 0, coef, alpha).T
    coef_column = columns[:, 0:1]
    alpha_column = columns[:, 1:2]
    for head in range(OWN_HEADS):
        mine = cond[head].astype(jnp.float32)
        span = slice(head * HEAD_DIM, (head + 1) * HEAD_DIM)
        diff = mine - uncond_ref[:, span].astype(jnp.float32)
        steered = mine + alpha_column * (diff - coef_column * mine)
        out_ref[:, span] = steered.astype(jnp.bfloat16)

    for step in range(1, tensor_size):
        tell(step).wait_send()
    for kind in kinds:
        push(kind, 1, SEQ + 1 - half, far).wait_send()

        @pl.when(jnp.logical_not(has_extra))
        def _():
            push(kind, 1, SEQ + half, near).wait_send()

        for peer in peers:
            push(kind, 0, peer, peer).wait_send()
    for peer in peers:
        give_back(0, z, peer).wait_send()

    @pl.when(has_extra)
    def _():
        for peer in peers:
            give_back(1, SEQ + half, peer).wait_send()


def exchanged(
    tensor_size,
    queries, keys, values, text_keys, text_values, text_len, uncond, flags, guide_num, guide_den
):
    rows, width = queries.shape
    text_rows = text_keys.shape[0]
    joint = SEQ * (rows + text_rows)
    hbm = pl.BlockSpec(memory_space=pl.ANY)
    vmem = pl.BlockSpec(memory_space=pltpu.VMEM)
    smem = pl.BlockSpec(memory_space=pltpu.SMEM)
    dma = pltpu.SemaphoreType.DMA
    return pl.pallas_call(
        functools.partial(kernel, tensor_size),
        out_shape=jax.ShapeDtypeStruct((rows, width), jnp.bfloat16),
        in_specs=[hbm] * 5 + [smem, vmem, vmem, smem, smem],
        out_specs=vmem,
        scratch_shapes=[
            pltpu.VMEM((2, SEQ * rows, HEAD_DIM), jnp.bfloat16),
            pltpu.VMEM((2, joint, HEAD_DIM), jnp.bfloat16),
            pltpu.VMEM((2, joint, HEAD_DIM), jnp.bfloat16),
            pltpu.VMEM((OWN_HEADS, rows, HEAD_DIM), jnp.bfloat16),
            pltpu.VMEM((8, rows), jnp.float32),
            pltpu.VMEM((tensor_size - 1, 8, rows), jnp.float32),
            dma((2, 5)),
            dma((2, 5, SEQ)),
            dma((2, 5, SEQ)),
            dma((2, SEQ)),
            dma((OWN_HEADS,)),
            dma((tensor_size - 1,)),
            dma((tensor_size - 1,)),
        ],
        compiler_params=pltpu.CompilerParams(
            collective_id=0, has_side_effects=True, vmem_limit_bytes=40 * 1024 * 1024
        ),
        cost_estimate=pl.CostEstimate(
            flops=4 * rows * joint * width,
            bytes_accessed=10 * rows * width,
            transcendentals=rows * joint * OWN_HEADS,
        ),
    )(
        queries, keys, values, text_keys, text_values, text_len, uncond,
        flags.reshape(1, rows), guide_num, guide_den,
    )


def local(
    queries, keys, values, text_keys, text_values, text_len, uncond, flags, guide_num, guide_den
):
    tok_rows, width = queries.shape
    heads = width // HEAD_DIM
    factor = 1.0 / math.sqrt(HEAD_DIM)
    limit = text_len[0]

    def attend(state, query_heads, key_piece, value_piece, live):
        rows = key_piece.shape[0]
        key_heads = key_piece.reshape(rows, heads, HEAD_DIM)
        value_heads = value_piece.reshape(rows, heads, HEAD_DIM)
        scores = (
            jnp.einsum("qhd,khd->hqk", query_heads, key_heads, preferred_element_type=jnp.float32)
            * factor
        )
        if live is not None:
            scores = jnp.where(live[None, None, :], scores, -1e30)
        top, total, accum = state
        new_top = jnp.maximum(top, jnp.max(scores, axis=2))
        fade = jnp.exp(top - new_top)
        weights = jnp.exp(scores - new_top[:, :, None])
        total = total * fade + jnp.sum(weights, axis=2)
        mixed = jnp.einsum(
            "hqk,khd->hqd",
            weights.astype(jnp.bfloat16),
            value_heads,
            preferred_element_type=jnp.float32,
        )
        accum = accum * fade[:, :, None] + mixed
        return (new_top, total, accum)

    def blocked(state, query_heads, key_piece, value_piece, block):
        rows = key_piece.shape[0]
        if rows <= block or rows % block != 0:
            return attend(state, query_heads, key_piece, value_piece, None)
        key_blocks = key_piece.reshape(rows // block, block, width)
        value_blocks = value_piece.reshape(rows // block, block, width)

        def step_block(carry, pair):
            return (attend(carry, query_heads, pair[0], pair[1], None), None)

        return lax.scan(step_block, state, (key_blocks, value_blocks))[0]

    query_heads = queries.reshape(tok_rows, heads, HEAD_DIM)
    state = blocked(
        (
            jnp.full((heads, tok_rows), -1e30, jnp.float32),
            jnp.zeros((heads, tok_rows), jnp.float32),
            jnp.zeros((heads, tok_rows, HEAD_DIM), jnp.float32),
        ),
        query_heads,
        lax.all_gather(keys, "seq", axis=0, tiled=True),
        lax.all_gather(values, "seq", axis=0, tiled=True),
        1024,
    )
    all_text_keys, all_text_values = (
        lax.all_gather(text_keys, "seq", axis=0, tiled=True),
        lax.all_gather(text_values, "seq", axis=0, tiled=True),
    )
    text_live = jnp.arange(all_text_keys.shape[0]) < limit
    state = attend(state, query_heads, all_text_keys, all_text_values, text_live)
    top, total, accum = state
    cond = (accum / total[:, :, None]).transpose(1, 0, 2).reshape(tok_rows, width)
    diff = cond - uncond.astype(jnp.float32)
    inner, square = lax.psum((jnp.sum(diff * cond, axis=1), jnp.sum(cond * cond, axis=1)), "tensor")
    full_width = width * lax.axis_size("tensor")
    coef = inner / full_width / (square / full_width + 1e-06)
    scale = guide_num[0].astype(jnp.float32) / guide_den[0].astype(jnp.float32)
    steered = cond + (scale - 1.0) * (diff - coef[:, None] * cond)
    return jnp.where(flags[:, None] > 0, steered, cond).astype(jnp.bfloat16)


def solution(mesh):
    tensor_size = mesh.shape["tensor"]

    def pick(queries, *rest):
        fits = (
            mesh.shape["seq"] == SEQ
            and tensor_size % 2 == 0
            and queries.shape[1] == OWN_HEADS * HEAD_DIM
        )
        if fits:
            return exchanged(tensor_size, queries, *rest)
        return local(queries, *rest)

    return jax.shard_map(
        pick,
        mesh=mesh,
        in_specs=(
            P(("groups", "seq"), "tensor"),
            P(("groups", "seq"), "tensor"),
            P(("groups", "seq"), "tensor"),
            P(("groups", "seq"), "tensor"),
            P(("groups", "seq"), "tensor"),
            P("groups"),
            P(("groups", "seq"), "tensor"),
            P(("groups", "seq")),
            P("groups"),
            P("groups"),
        ),
        out_specs=P(("groups", "seq"), "tensor"),
        check_vma=False,
    )
```

```python
import functools
import math

import jax
import jax.numpy as jnp
from jax import lax
from jax.experimental import pallas as pl
from jax.experimental.pallas import tpu as pltpu
from jax.sharding import PartitionSpec as P

HEAD_DIM = 128
SEQ = 4
OWN_HEADS = 6
MESH = pl.DeviceIdType.MESH
K, V, TK, TV, Q = range(5)


def kernel(
    tensor_size,
    q_hbm, k_hbm, v_hbm, tk_hbm, tv_hbm, len_ref, uncond_hbm, flags_hbm, num_ref, den_ref,
    out_ref,
    qs, ks, vs, cond, sums, stats, uncond_ref, flags_ref,
    side_sem, own_sem, send_sem, recv_sem, back_send, back_recv, stat_send, stat_recv,
):
    rows = q_hbm.shape[0]
    text_rows = tk_hbm.shape[0]
    tokens = SEQ * rows
    group = lax.axis_index("groups")
    z = lax.axis_index("seq")
    t = lax.axis_index("tensor")
    core = lax.rem(t, 2)
    half = z // 2
    peers = (lax.rem(z + 2, SEQ), SEQ - 1 - z, z + 1 - 2 * lax.rem(z, 2))
    has_extra = lax.rem(z, 2) == core

    def at(seq, tensor):
        return (group, seq, tensor)

    sources = {K: k_hbm, V: v_hbm, TK: tk_hbm, TV: tv_hbm, Q: q_hbm}

    def place(kind, slot, source):
        if kind == Q:
            return qs.at[slot, pl.ds(source * rows, rows), :]
        big = ks if kind in (K, TK) else vs
        if kind in (K, V):
            return big.at[slot, pl.ds(source * rows, rows), :]
        return big.at[slot, pl.ds(tokens + source * text_rows, text_rows), :]

    def column(head):
        return pl.ds(pl.multiple_of(head * HEAD_DIM, HEAD_DIM), HEAD_DIM)

    def push(kind, slot, head, target):
        return pltpu.make_async_remote_copy(
            src_ref=sources[kind].at[:, column(head)],
            dst_ref=place(kind, slot, z),
            send_sem=send_sem.at[slot, kind, target],
            recv_sem=recv_sem.at[slot, kind, z],
            device_id=at(target, t),
            device_id_type=MESH,
        )

    def arrival(kind, slot, source):
        return pltpu.make_async_remote_copy(
            src_ref=place(kind, slot, source),
            dst_ref=place(kind, slot, source),
            send_sem=send_sem.at[slot, kind, source],
            recv_sem=recv_sem.at[slot, kind, source],
            device_id=at(source, t),
            device_id_type=MESH,
        )

    def keep(kind, slot, head):
        return pltpu.make_async_copy(
            sources[kind].at[:, column(head)], place(kind, slot, z), own_sem.at[slot, kind]
        )

    def give_back(slot, head, target):
        return pltpu.make_async_remote_copy(
            src_ref=qs.at[slot, pl.ds(target * rows, rows), :],
            dst_ref=cond.at[head],
            send_sem=back_send.at[slot, target],
            recv_sem=back_recv.at[head],
            device_id=at(target, t),
            device_id_type=MESH,
        )

    side = [
        pltpu.make_async_copy(source, target, side_sem.at[index])
        for index, (source, target) in enumerate(
            (
                (flags_hbm, flags_ref),
                (uncond_hbm, uncond_ref),
            )
        )
    ]
    kinds = (K, TK, V, TV, Q)

    barrier = pltpu.get_barrier_semaphore()
    for peer in peers:
        pl.semaphore_signal(barrier, inc=1, device_id=at(peer, t), device_id_type=MESH)
    others = [lax.rem(t + step, tensor_size) for step in range(1, tensor_size)]
    for other in others:
        pl.semaphore_signal(barrier, inc=1, device_id=at(z, other), device_id_type=MESH)
    pl.semaphore_wait(barrier, len(peers) + len(others))

    far = 2 * (1 - half) + core
    near = 2 * half + core
    for kind in kinds:
        push(kind, 1, SEQ + 1 - half, far).start()

        @pl.when(jnp.logical_not(has_extra))
        def _():
            push(kind, 1, SEQ + half, near).start()

    for kind in kinds:
        for peer in peers:
            push(kind, 0, peer, peer).start()

    for copy in side:
        copy.start()

    @pl.when(has_extra)
    def _():
        for kind in kinds:
            keep(kind, 1, SEQ + half).start()

    for kind in kinds:
        keep(kind, 0, z).start()

    scale_log2 = math.log2(math.e) / math.sqrt(HEAD_DIM)
    live = lax.broadcasted_iota(jnp.int32, (rows, SEQ * text_rows), 1) < len_ref[0]
    contract = (((1,), (1,)), ((), ()))

    def attend(slot, source, head):
        query = qs[slot, pl.ds(source * rows, rows), :]
        image = lax.dot_general(
            query, ks[slot, pl.ds(0, tokens), :], contract, preferred_element_type=jnp.float32
        )
        text = lax.dot_general(
            query,
            ks[slot, pl.ds(tokens, SEQ * text_rows), :],
            contract,
            preferred_element_type=jnp.float32,
        )
        text = jnp.where(live, text * scale_log2, -1e30)
        image = image * scale_log2
        top = jnp.maximum(
            jnp.max(image, axis=1, keepdims=True), jnp.max(text, axis=1, keepdims=True)
        )
        image = jnp.exp2(image - top)
        text = jnp.exp2(text - top)
        total = jnp.sum(image, axis=1, keepdims=True) + jnp.sum(text, axis=1, keepdims=True)
        mixed = jnp.dot(
            image.astype(jnp.bfloat16),
            vs[slot, pl.ds(0, tokens), :],
            preferred_element_type=jnp.float32,
        ) + jnp.dot(
            text.astype(jnp.bfloat16),
            vs[slot, pl.ds(tokens, SEQ * text_rows), :],
            preferred_element_type=jnp.float32,
        )
        return (mixed / total).astype(jnp.bfloat16)

    def work(slot, head):
        for kind in (K, TK, V, TV):
            keep(kind, slot, head).wait()
            for peer in peers:
                arrival(kind, slot, peer).wait_recv()
        keep(Q, slot, head).wait()
        cond[head] = attend(slot, z, head)
        for peer in peers:
            arrival(Q, slot, peer).wait_recv()
            result = attend(slot, peer, head)
            qs[slot, pl.ds(peer * rows, rows), :] = result
            give_back(slot, head, peer).start()

    @pl.when(has_extra)
    def _():
        work(1, SEQ + half)

    work(0, z)

    def landed(head, source):
        return pltpu.make_async_remote_copy(
            src_ref=cond.at[head],
            dst_ref=cond.at[head],
            send_sem=back_send.at[0, source],
            recv_sem=back_recv.at[head],
            device_id=at(source, t),
            device_id_type=MESH,
        )

    for copy in side:
        copy.wait()
    landed(SEQ + 1 - half, far).wait_recv()

    @pl.when(jnp.logical_not(has_extra))
    def _():
        landed(SEQ + half, near).wait_recv()

    for peer in peers:
        landed(peer, peer).wait_recv()

    inner = jnp.zeros((rows, HEAD_DIM), jnp.float32)
    square = jnp.zeros((rows, HEAD_DIM), jnp.float32)
    for head in range(OWN_HEADS):
        mine = cond[head].astype(jnp.float32)
        diff = mine - uncond_ref[:, head * HEAD_DIM : (head + 1) * HEAD_DIM].astype(jnp.float32)
        inner += diff * mine
        square += mine * mine
    lane = lax.broadcasted_iota(jnp.int32, (rows, HEAD_DIM), 1)
    pair = jnp.where(
        lane == 0,
        jnp.sum(inner, axis=1, keepdims=True),
        jnp.sum(square, axis=1, keepdims=True),
    )
    sums[...] = pair.T[0:8, :]

    def tell(step):
        return pltpu.make_async_remote_copy(
            src_ref=sums,
            dst_ref=stats.at[step - 1],
            send_sem=stat_send.at[step - 1],
            recv_sem=stat_recv.at[step - 1],
            device_id=at(z, lax.rem(t + step, tensor_size)),
            device_id_type=MESH,
        )

    for step in range(1, tensor_size):
        tell(step).start()
    both = sums[...]
    for step in range(1, tensor_size):
        tell(step).wait_recv()
        both = both + stats[step - 1]
    width = tensor_size * OWN_HEADS * HEAD_DIM
    coef = both[0:1, :] / width / (both[1:2, :] / width + 1e-6)
    scale = num_ref[0].astype(jnp.float32) / den_ref[0].astype(jnp.float32)
    alpha = jnp.where(flags_ref[...] > 0, scale - 1.0, 0.0)
    line = lax.broadcasted_iota(jnp.int32, (HEAD_DIM, rows), 0)
    columns = jnp.where(line == 0, coef, alpha).T
    coef_column = columns[:, 0:1]
    alpha_column = columns[:, 1:2]
    for head in range(OWN_HEADS):
        mine = cond[head].astype(jnp.float32)
        span = slice(head * HEAD_DIM, (head + 1) * HEAD_DIM)
        diff = mine - uncond_ref[:, span].astype(jnp.float32)
        steered = mine + alpha_column * (diff - coef_column * mine)
        out_ref[:, span] = steered.astype(jnp.bfloat16)

    for step in range(1, tensor_size):
        tell(step).wait_send()
    for kind in kinds:
        push(kind, 1, SEQ + 1 - half, far).wait_send()

        @pl.when(jnp.logical_not(has_extra))
        def _():
            push(kind, 1, SEQ + half, near).wait_send()

        for peer in peers:
            push(kind, 0, peer, peer).wait_send()
    for peer in peers:
        give_back(0, z, peer).wait_send()

    @pl.when(has_extra)
    def _():
        for peer in peers:
            give_back(1, SEQ + half, peer).wait_send()


def exchanged(
    tensor_size,
    queries, keys, values, text_keys, text_values, text_len, uncond, flags, guide_num, guide_den
):
    rows, width = queries.shape
    text_rows = text_keys.shape[0]
    joint = SEQ * (rows + text_rows)
    hbm = pl.BlockSpec(memory_space=pl.ANY)
    vmem = pl.BlockSpec(memory_space=pltpu.VMEM)
    smem = pl.BlockSpec(memory_space=pltpu.SMEM)
    dma = pltpu.SemaphoreType.DMA
    return pl.pallas_call(
        functools.partial(kernel, tensor_size),
        out_shape=jax.ShapeDtypeStruct((rows, width), jnp.bfloat16),
        in_specs=[hbm] * 5 + [smem, hbm, hbm, smem, smem],
        out_specs=vmem,
        scratch_shapes=[
            pltpu.VMEM((2, SEQ * rows, HEAD_DIM), jnp.bfloat16),
            pltpu.VMEM((2, joint, HEAD_DIM), jnp.bfloat16),
            pltpu.VMEM((2, joint, HEAD_DIM), jnp.bfloat16),
            pltpu.VMEM((OWN_HEADS, rows, HEAD_DIM), jnp.bfloat16),
            pltpu.VMEM((8, rows), jnp.float32),
            pltpu.VMEM((tensor_size - 1, 8, rows), jnp.float32),
            pltpu.VMEM((rows, width), jnp.bfloat16),
            pltpu.VMEM((1, rows), jnp.int32),
            dma((2,)),
            dma((2, 5)),
            dma((2, 5, SEQ)),
            dma((2, 5, SEQ)),
            dma((2, SEQ)),
            dma((OWN_HEADS,)),
            dma((tensor_size - 1,)),
            dma((tensor_size - 1,)),
        ],
        compiler_params=pltpu.CompilerParams(
            collective_id=0, has_side_effects=True, vmem_limit_bytes=60 * 1024 * 1024
        ),
        cost_estimate=pl.CostEstimate(
            flops=4 * rows * joint * width,
            bytes_accessed=10 * rows * width,
            transcendentals=rows * joint * OWN_HEADS,
        ),
    )(
        queries, keys, values, text_keys, text_values, text_len, uncond,
        flags.reshape(1, rows), guide_num, guide_den,
    )


def local(
    queries, keys, values, text_keys, text_values, text_len, uncond, flags, guide_num, guide_den
):
    tok_rows, width = queries.shape
    heads = width // HEAD_DIM
    factor = 1.0 / math.sqrt(HEAD_DIM)
    limit = text_len[0]

    def attend(state, query_heads, key_piece, value_piece, live):
        rows = key_piece.shape[0]
        key_heads = key_piece.reshape(rows, heads, HEAD_DIM)
        value_heads = value_piece.reshape(rows, heads, HEAD_DIM)
        scores = (
            jnp.einsum("qhd,khd->hqk", query_heads, key_heads, preferred_element_type=jnp.float32)
            * factor
        )
        if live is not None:
            scores = jnp.where(live[None, None, :], scores, -1e30)
        top, total, accum = state
        new_top = jnp.maximum(top, jnp.max(scores, axis=2))
        fade = jnp.exp(top - new_top)
        weights = jnp.exp(scores - new_top[:, :, None])
        total = total * fade + jnp.sum(weights, axis=2)
        mixed = jnp.einsum(
            "hqk,khd->hqd",
            weights.astype(jnp.bfloat16),
            value_heads,
            preferred_element_type=jnp.float32,
        )
        accum = accum * fade[:, :, None] + mixed
        return (new_top, total, accum)

    def blocked(state, query_heads, key_piece, value_piece, block):
        rows = key_piece.shape[0]
        if rows <= block or rows % block != 0:
            return attend(state, query_heads, key_piece, value_piece, None)
        key_blocks = key_piece.reshape(rows // block, block, width)
        value_blocks = value_piece.reshape(rows // block, block, width)

        def step_block(carry, pair):
            return (attend(carry, query_heads, pair[0], pair[1], None), None)

        return lax.scan(step_block, state, (key_blocks, value_blocks))[0]

    query_heads = queries.reshape(tok_rows, heads, HEAD_DIM)
    state = blocked(
        (
            jnp.full((heads, tok_rows), -1e30, jnp.float32),
            jnp.zeros((heads, tok_rows), jnp.float32),
            jnp.zeros((heads, tok_rows, HEAD_DIM), jnp.float32),
        ),
        query_heads,
        lax.all_gather(keys, "seq", axis=0, tiled=True),
        lax.all_gather(values, "seq", axis=0, tiled=True),
        1024,
    )
    all_text_keys, all_text_values = (
        lax.all_gather(text_keys, "seq", axis=0, tiled=True),
        lax.all_gather(text_values, "seq", axis=0, tiled=True),
    )
    text_live = jnp.arange(all_text_keys.shape[0]) < limit
    state = attend(state, query_heads, all_text_keys, all_text_values, text_live)
    top, total, accum = state
    cond = (accum / total[:, :, None]).transpose(1, 0, 2).reshape(tok_rows, width)
    diff = cond - uncond.astype(jnp.float32)
    inner, square = lax.psum((jnp.sum(diff * cond, axis=1), jnp.sum(cond * cond, axis=1)), "tensor")
    full_width = width * lax.axis_size("tensor")
    coef = inner / full_width / (square / full_width + 1e-06)
    scale = guide_num[0].astype(jnp.float32) / guide_den[0].astype(jnp.float32)
    steered = cond + (scale - 1.0) * (diff - coef[:, None] * cond)
    return jnp.where(flags[:, None] > 0, steered, cond).astype(jnp.bfloat16)


def solution(mesh):
    tensor_size = mesh.shape["tensor"]

    def pick(queries, *rest):
        fits = (
            mesh.shape["seq"] == SEQ
            and tensor_size % 2 == 0
            and queries.shape[1] == OWN_HEADS * HEAD_DIM
        )
        if fits:
            return exchanged(tensor_size, queries, *rest)
        return local(queries, *rest)

    return jax.shard_map(
        pick,
        mesh=mesh,
        in_specs=(
            P(("groups", "seq"), "tensor"),
            P(("groups", "seq"), "tensor"),
            P(("groups", "seq"), "tensor"),
            P(("groups", "seq"), "tensor"),
            P(("groups", "seq"), "tensor"),
            P("groups"),
            P(("groups", "seq"), "tensor"),
            P(("groups", "seq")),
            P("groups"),
            P("groups"),
        ),
        out_specs=P(("groups", "seq"), "tensor"),
        check_vma=False,
    )
```

```python
import functools
import math

import jax
import jax.numpy as jnp
from jax import lax
from jax.experimental import pallas as pl
from jax.experimental.pallas import tpu as pltpu
from jax.sharding import PartitionSpec as P

HEAD_DIM = 128
SEQ = 4
OWN_HEADS = 6
MESH = pl.DeviceIdType.MESH
K, V, TK, TV, Q = range(5)


def kernel(
    tensor_size,
    q_hbm, k_hbm, v_hbm, tk_hbm, tv_hbm, len_ref, uncond_hbm, flags_hbm, num_ref, den_ref,
    out_ref,
    qs, ks, vs, cond, sums, stats, uncond_ref, flags_ref,
    side_sem, own_sem, send_sem, recv_sem, back_send, back_recv, stat_send, stat_recv,
):
    rows = q_hbm.shape[0]
    text_rows = tk_hbm.shape[0]
    tokens = SEQ * rows
    group = lax.axis_index("groups")
    z = lax.axis_index("seq")
    t = lax.axis_index("tensor")
    core = lax.rem(t, 2)
    half = z // 2
    peers = (lax.rem(z + 2, SEQ), SEQ - 1 - z, z + 1 - 2 * lax.rem(z, 2))
    has_extra = lax.rem(z, 2) == core

    def at(seq, tensor):
        return (group, seq, tensor)

    sources = {K: k_hbm, V: v_hbm, TK: tk_hbm, TV: tv_hbm, Q: q_hbm}

    def place(kind, slot, source):
        if kind == Q:
            return qs.at[slot, pl.ds(source * rows, rows), :]
        big = ks if kind in (K, TK) else vs
        if kind in (K, V):
            return big.at[slot, pl.ds(source * rows, rows), :]
        return big.at[slot, pl.ds(tokens + source * text_rows, text_rows), :]

    def column(head):
        return pl.ds(pl.multiple_of(head * HEAD_DIM, HEAD_DIM), HEAD_DIM)

    def push(kind, slot, head, target):
        return pltpu.make_async_remote_copy(
            src_ref=sources[kind].at[:, column(head)],
            dst_ref=place(kind, slot, z),
            send_sem=send_sem.at[slot, kind, target],
            recv_sem=recv_sem.at[slot, kind, z],
            device_id=at(target, t),
            device_id_type=MESH,
        )

    def arrival(kind, slot, source):
        return pltpu.make_async_remote_copy(
            src_ref=place(kind, slot, source),
            dst_ref=place(kind, slot, source),
            send_sem=send_sem.at[slot, kind, source],
            recv_sem=recv_sem.at[slot, kind, source],
            device_id=at(source, t),
            device_id_type=MESH,
        )

    def keep(kind, slot, head):
        return pltpu.make_async_copy(
            sources[kind].at[:, column(head)], place(kind, slot, z), own_sem.at[slot, kind]
        )

    def give_back(slot, head, target):
        return pltpu.make_async_remote_copy(
            src_ref=qs.at[slot, pl.ds(target * rows, rows), :],
            dst_ref=cond.at[head],
            send_sem=back_send.at[slot, target],
            recv_sem=back_recv.at[head],
            device_id=at(target, t),
            device_id_type=MESH,
        )

    side = [
        pltpu.make_async_copy(source, target, side_sem.at[index])
        for index, (source, target) in enumerate(
            (
                (flags_hbm, flags_ref),
                (uncond_hbm, uncond_ref),
            )
        )
    ]
    kinds = (K, TK, V, TV, Q)

    barrier = pltpu.get_barrier_semaphore()
    for peer in peers:
        pl.semaphore_signal(barrier, inc=1, device_id=at(peer, t), device_id_type=MESH)
    others = [lax.rem(t + step, tensor_size) for step in range(1, tensor_size)]
    for other in others:
        pl.semaphore_signal(barrier, inc=1, device_id=at(z, other), device_id_type=MESH)
    pl.semaphore_wait(barrier, len(peers) + len(others))

    far = 2 * (1 - half) + core
    near = 2 * half + core
    for kind in kinds:
        push(kind, 1, SEQ + 1 - half, far).start()

        @pl.when(jnp.logical_not(has_extra))
        def _():
            push(kind, 1, SEQ + half, near).start()

    for kind in kinds:
        for peer in peers:
            push(kind, 0, peer, peer).start()

    for copy in side:
        copy.start()

    @pl.when(has_extra)
    def _():
        for kind in kinds:
            keep(kind, 1, SEQ + half).start()

    for kind in kinds:
        keep(kind, 0, z).start()

    scale_log2 = math.log2(math.e) / math.sqrt(HEAD_DIM)
    live = lax.broadcasted_iota(jnp.int32, (rows, SEQ * text_rows), 1) < len_ref[0]
    contract = (((1,), (1,)), ((), ()))

    def attend(slot, source, head):
        query = qs[slot, pl.ds(source * rows, rows), :]
        image = lax.dot_general(
            query, ks[slot, pl.ds(0, tokens), :], contract, preferred_element_type=jnp.float32
        )
        text = lax.dot_general(
            query,
            ks[slot, pl.ds(tokens, SEQ * text_rows), :],
            contract,
            preferred_element_type=jnp.float32,
        )
        text = jnp.where(live, text * scale_log2, -1e30)
        image = image * scale_log2
        top = jnp.maximum(
            jnp.max(image, axis=1, keepdims=True), jnp.max(text, axis=1, keepdims=True)
        )
        image = jnp.exp2(image - top)
        text = jnp.exp2(text - top)
        total = jnp.sum(image, axis=1, keepdims=True) + jnp.sum(text, axis=1, keepdims=True)
        mixed = jnp.dot(
            image.astype(jnp.bfloat16),
            vs[slot, pl.ds(0, tokens), :],
            preferred_element_type=jnp.float32,
        ) + jnp.dot(
            text.astype(jnp.bfloat16),
            vs[slot, pl.ds(tokens, SEQ * text_rows), :],
            preferred_element_type=jnp.float32,
        )
        return (mixed / total).astype(jnp.bfloat16)

    def work(slot, head):
        for kind in (K, TK, V, TV):
            keep(kind, slot, head).wait()
            for peer in peers:
                arrival(kind, slot, peer).wait_recv()
        for peer in peers:
            arrival(Q, slot, peer).wait_recv()
            result = attend(slot, peer, head)
            qs[slot, pl.ds(peer * rows, rows), :] = result
            give_back(slot, head, peer).start()
        keep(Q, slot, head).wait()
        cond[head] = attend(slot, z, head)

    @pl.when(has_extra)
    def _():
        work(1, SEQ + half)

    work(0, z)

    def landed(head, source):
        return pltpu.make_async_remote_copy(
            src_ref=cond.at[head],
            dst_ref=cond.at[head],
            send_sem=back_send.at[0, source],
            recv_sem=back_recv.at[head],
            device_id=at(source, t),
            device_id_type=MESH,
        )

    for copy in side:
        copy.wait()
    def add_up(head, so_far):
        inner, square = so_far
        mine = cond[head].astype(jnp.float32)
        other = uncond_ref[:, column(head)].astype(jnp.float32)
        return inner + (mine - other) * mine, square + mine * mine

    zero = jnp.zeros((rows, HEAD_DIM), jnp.float32)
    so_far = add_up(z, (zero, zero))
    landed(SEQ + 1 - half, far).wait_recv()
    so_far = add_up(SEQ + 1 - half, so_far)

    @pl.when(jnp.logical_not(has_extra))
    def _():
        landed(SEQ + half, near).wait_recv()

    so_far = add_up(SEQ + half, so_far)
    for peer in peers:
        landed(peer, peer).wait_recv()
        so_far = add_up(peer, so_far)
    inner, square = so_far
    lane = lax.broadcasted_iota(jnp.int32, (rows, HEAD_DIM), 1)
    pair = jnp.where(
        lane == 0,
        jnp.sum(inner, axis=1, keepdims=True),
        jnp.sum(square, axis=1, keepdims=True),
    )
    sums[...] = pair.T[0:8, :]

    def tell(step):
        return pltpu.make_async_remote_copy(
            src_ref=sums,
            dst_ref=stats.at[step - 1],
            send_sem=stat_send.at[step - 1],
            recv_sem=stat_recv.at[step - 1],
            device_id=at(z, lax.rem(t + step, tensor_size)),
            device_id_type=MESH,
        )

    for step in range(1, tensor_size):
        tell(step).start()
    both = sums[...]
    for step in range(1, tensor_size):
        tell(step).wait_recv()
        both = both + stats[step - 1]
    width = tensor_size * OWN_HEADS * HEAD_DIM
    coef = both[0:1, :] / width / (both[1:2, :] / width + 1e-6)
    scale = num_ref[0].astype(jnp.float32) / den_ref[0].astype(jnp.float32)
    alpha = jnp.where(flags_ref[...] > 0, scale - 1.0, 0.0)
    line = lax.broadcasted_iota(jnp.int32, (HEAD_DIM, rows), 0)
    columns = jnp.where(line == 0, coef, alpha).T
    coef_column = columns[:, 0:1]
    alpha_column = columns[:, 1:2]
    for head in range(OWN_HEADS):
        mine = cond[head].astype(jnp.float32)
        span = slice(head * HEAD_DIM, (head + 1) * HEAD_DIM)
        diff = mine - uncond_ref[:, span].astype(jnp.float32)
        steered = mine + alpha_column * (diff - coef_column * mine)
        out_ref[:, span] = steered.astype(jnp.bfloat16)

    for step in range(1, tensor_size):
        tell(step).wait_send()
    for kind in kinds:
        push(kind, 1, SEQ + 1 - half, far).wait_send()

        @pl.when(jnp.logical_not(has_extra))
        def _():
            push(kind, 1, SEQ + half, near).wait_send()

        for peer in peers:
            push(kind, 0, peer, peer).wait_send()
    for peer in peers:
        give_back(0, z, peer).wait_send()

    @pl.when(has_extra)
    def _():
        for peer in peers:
            give_back(1, SEQ + half, peer).wait_send()


def pinned(*arrays):
    return [pltpu.with_memory_space_constraint(array, pltpu.HBM) for array in arrays]


def exchanged(
    tensor_size,
    queries, keys, values, text_keys, text_values, text_len, uncond, flags, guide_num, guide_den
):
    rows, width = queries.shape
    text_rows = text_keys.shape[0]
    joint = SEQ * (rows + text_rows)
    hbm = pl.BlockSpec(memory_space=pltpu.HBM)
    vmem = pl.BlockSpec(memory_space=pltpu.VMEM)
    smem = pl.BlockSpec(memory_space=pltpu.SMEM)
    dma = pltpu.SemaphoreType.DMA
    return pl.pallas_call(
        functools.partial(kernel, tensor_size),
        out_shape=jax.ShapeDtypeStruct((rows, width), jnp.bfloat16),
        in_specs=[hbm] * 5 + [smem, hbm, hbm, smem, smem],
        out_specs=vmem,
        scratch_shapes=[
            pltpu.VMEM((2, SEQ * rows, HEAD_DIM), jnp.bfloat16),
            pltpu.VMEM((2, joint, HEAD_DIM), jnp.bfloat16),
            pltpu.VMEM((2, joint, HEAD_DIM), jnp.bfloat16),
            pltpu.VMEM((OWN_HEADS, rows, HEAD_DIM), jnp.bfloat16),
            pltpu.VMEM((8, rows), jnp.float32),
            pltpu.VMEM((tensor_size - 1, 8, rows), jnp.float32),
            pltpu.VMEM((rows, width), jnp.bfloat16),
            pltpu.VMEM((1, rows), jnp.int32),
            dma((2,)),
            dma((2, 5)),
            dma((2, 5, SEQ)),
            dma((2, 5, SEQ)),
            dma((2, SEQ)),
            dma((OWN_HEADS,)),
            dma((tensor_size - 1,)),
            dma((tensor_size - 1,)),
        ],
        compiler_params=pltpu.CompilerParams(
            collective_id=0, has_side_effects=True, vmem_limit_bytes=48 * 1024 * 1024
        ),
        cost_estimate=pl.CostEstimate(
            flops=4 * rows * joint * width,
            bytes_accessed=10 * rows * width,
            transcendentals=rows * joint * OWN_HEADS,
        ),
    )(
        *pinned(queries, keys, values, text_keys, text_values), text_len,
        *pinned(uncond, flags.reshape(1, rows)), guide_num, guide_den,
    )


def local(
    queries, keys, values, text_keys, text_values, text_len, uncond, flags, guide_num, guide_den
):
    tok_rows, width = queries.shape
    heads = width // HEAD_DIM
    factor = 1.0 / math.sqrt(HEAD_DIM)
    limit = text_len[0]

    def attend(state, query_heads, key_piece, value_piece, live):
        rows = key_piece.shape[0]
        key_heads = key_piece.reshape(rows, heads, HEAD_DIM)
        value_heads = value_piece.reshape(rows, heads, HEAD_DIM)
        scores = (
            jnp.einsum("qhd,khd->hqk", query_heads, key_heads, preferred_element_type=jnp.float32)
            * factor
        )
        if live is not None:
            scores = jnp.where(live[None, None, :], scores, -1e30)
        top, total, accum = state
        new_top = jnp.maximum(top, jnp.max(scores, axis=2))
        fade = jnp.exp(top - new_top)
        weights = jnp.exp(scores - new_top[:, :, None])
        total = total * fade + jnp.sum(weights, axis=2)
        mixed = jnp.einsum(
            "hqk,khd->hqd",
            weights.astype(jnp.bfloat16),
            value_heads,
            preferred_element_type=jnp.float32,
        )
        accum = accum * fade[:, :, None] + mixed
        return (new_top, total, accum)

    def blocked(state, query_heads, key_piece, value_piece, block):
        rows = key_piece.shape[0]
        if rows <= block or rows % block != 0:
            return attend(state, query_heads, key_piece, value_piece, None)
        key_blocks = key_piece.reshape(rows // block, block, width)
        value_blocks = value_piece.reshape(rows // block, block, width)

        def step_block(carry, pair):
            return (attend(carry, query_heads, pair[0], pair[1], None), None)

        return lax.scan(step_block, state, (key_blocks, value_blocks))[0]

    query_heads = queries.reshape(tok_rows, heads, HEAD_DIM)
    state = blocked(
        (
            jnp.full((heads, tok_rows), -1e30, jnp.float32),
            jnp.zeros((heads, tok_rows), jnp.float32),
            jnp.zeros((heads, tok_rows, HEAD_DIM), jnp.float32),
        ),
        query_heads,
        lax.all_gather(keys, "seq", axis=0, tiled=True),
        lax.all_gather(values, "seq", axis=0, tiled=True),
        1024,
    )
    all_text_keys, all_text_values = (
        lax.all_gather(text_keys, "seq", axis=0, tiled=True),
        lax.all_gather(text_values, "seq", axis=0, tiled=True),
    )
    text_live = jnp.arange(all_text_keys.shape[0]) < limit
    state = attend(state, query_heads, all_text_keys, all_text_values, text_live)
    top, total, accum = state
    cond = (accum / total[:, :, None]).transpose(1, 0, 2).reshape(tok_rows, width)
    diff = cond - uncond.astype(jnp.float32)
    inner, square = lax.psum((jnp.sum(diff * cond, axis=1), jnp.sum(cond * cond, axis=1)), "tensor")
    full_width = width * lax.axis_size("tensor")
    coef = inner / full_width / (square / full_width + 1e-06)
    scale = guide_num[0].astype(jnp.float32) / guide_den[0].astype(jnp.float32)
    steered = cond + (scale - 1.0) * (diff - coef[:, None] * cond)
    return jnp.where(flags[:, None] > 0, steered, cond).astype(jnp.bfloat16)


def solution(mesh):
    tensor_size = mesh.shape["tensor"]

    def pick(queries, *rest):
        fits = (
            mesh.shape["seq"] == SEQ
            and tensor_size % 2 == 0
            and queries.shape[1] == OWN_HEADS * HEAD_DIM
        )
        if fits:
            return exchanged(tensor_size, queries, *rest)
        return local(queries, *rest)

    return jax.shard_map(
        pick,
        mesh=mesh,
        in_specs=(
            P(("groups", "seq"), "tensor"),
            P(("groups", "seq"), "tensor"),
            P(("groups", "seq"), "tensor"),
            P(("groups", "seq"), "tensor"),
            P(("groups", "seq"), "tensor"),
            P("groups"),
            P(("groups", "seq"), "tensor"),
            P(("groups", "seq")),
            P("groups"),
            P("groups"),
        ),
        out_specs=P(("groups", "seq"), "tensor"),
        check_vma=False,
    )
```
